256 devices in a mesh: feat: 64 (over x, z_lo, y), dp: 4 (over z_hi, core).
Axes of the slice: x: 4, y: 4, z: 8 (z_hi: 2, z_lo: 4; z = z_hi * 4 + z_lo), core: 2. Of those that a mesh axis runs over, the one named last changes fastest.
Arguments:
- inputs: bfloat16 [1024, 65536], P('dp', 'feat'), may hold values from -6 to 6
- weights: bfloat16 [128, 8, 512, 512], P('feat'), may hold values from -0.09375 to 0.09375
- cotangent: bfloat16 [1024, 65536], P('dp', 'feat'), may hold values from -0.75 to 0.75
Outputs:
- outputs: bfloat16 [1024, 65536], P('dp', 'feat')
- input_grad: bfloat16 [1024, 65536], P('dp', 'feat')
- weight_grad: bfloat16 [128, 8, 512, 512], P('feat', None, 'dp')
The draws below stay inside these ranges and needn't reach their ends.
All inputs are finite; a program needn't handle non-finite values.
Results may differ from the reference program's by a relative error of at most 0.0047.
Values may be sent and summed in bfloat16 or wider, within the bound.
A program may use at most 128 MiB of HBM per device.

```python
import jax
import jax.numpy as jnp
from jax import lax

BLOCK = 512
NBLK = 128
LEVELS = 7
SLOTS = 8
WIDTH = 65536
TOKENS = 1024


def steps_of(rng, extent, shards, smallest, top_value):
    gain = 1.0
    for dim, shards_of in shards:
        steps = jax.random.uniform(jax.random.fold_in(jax.random.fold_in(rng, 6), dim), (shards_of,), jnp.float32, smallest / len(shards), top_value / len(shards))
        gain = gain * jnp.repeat(jnp.exp(steps), extent[dim] // shards_of).reshape((-1,) + (1,) * (len(extent) - 1 - dim))
    return gain


def gaussian(rng, dims, scale, bound, pieces=(), kind=jnp.bfloat16):
    gain = steps_of(rng, dims, pieces, -0.22, 0.18) if pieces else 1.0
    result = jax.random.normal(rng, dims, jnp.float32) * scale * gain
    return jnp.minimum(jnp.maximum(result, -bound), bound).astype(kind)


def setup_inputs(seed: int = 0) -> dict:
    key_of = jax.random.split(jax.random.key(seed), 4)
    return {
        "inputs": gaussian(key_of[0], (TOKENS, WIDTH), 1.0, 6.0, ((0, 4), (1, 64))),
        "weights": gaussian(key_of[1], (NBLK, SLOTS, BLOCK, BLOCK), (SLOTS * BLOCK) ** -0.5, 0.09375, ((0, 64),)),
        "cotangent": gaussian(key_of[2], (TOKENS, WIDTH), 0.125, 0.75, ((0, 4), (1, 64))),
    }


def reference(inputs, weights, cotangent):
    features = inputs.reshape(TOKENS, NBLK, BLOCK).astype(jnp.float32)
    upstream = cotangent.reshape(TOKENS, NBLK, BLOCK).astype(jnp.float32)
    shifts = jnp.left_shift(jnp.ones((LEVELS,), jnp.int32), jnp.arange(LEVELS, dtype=jnp.int32)).astype(jnp.int32)
    zero_index = jnp.zeros((), jnp.int32)

    def one_row(row_index):
        partners = jnp.concatenate([row_index[None], jnp.bitwise_xor(row_index, shifts)]).astype(jnp.int32)
        gathered = jnp.take(features, partners, axis=1)
        weight_row = lax.dynamic_index_in_dim(weights, row_index, 0, keepdims=False).astype(jnp.float32)
        mixed_rows = jnp.einsum("tsa,sab->tb", gathered, weight_row)
        own_grad = lax.dynamic_index_in_dim(upstream, row_index, 1, keepdims=False)
        weight_term = jnp.einsum("tsa,tb->sab", gathered, own_grad)
        back_total = jnp.einsum("tb,ab->ta", own_grad, weight_row[0])
        for slot_index in range(1, SLOTS):
            source = partners[slot_index]
            their_grad = lax.dynamic_index_in_dim(upstream, source, 1, keepdims=False)
            their_weight = lax.dynamic_slice(
                weights, (source, jnp.asarray(slot_index, jnp.int32), zero_index, zero_index),
                (1, 1, BLOCK, BLOCK)).reshape(BLOCK, BLOCK).astype(jnp.float32)
            partial_term = jnp.einsum("tb,ab->ta", their_grad, their_weight).astype(jnp.bfloat16)
            partial_term = lax.optimization_barrier(partial_term).astype(jnp.float32)
            back_total = back_total + partial_term
        return mixed_rows.astype(jnp.bfloat16), back_total.astype(jnp.bfloat16), weight_term.astype(jnp.bfloat16)

    results = lax.map(one_row, jnp.arange(NBLK, dtype=jnp.int32))
    outputs = jnp.transpose(results[0], (1, 0, 2)).reshape(TOKENS, WIDTH)
    input_grad = jnp.transpose(results[1], (1, 0, 2)).reshape(TOKENS, WIDTH)
    weight_grad = results[2]
    return outputs, input_grad, weight_grad
```

```python
import jax
import jax.numpy as jnp
from jax import lax
from jax.experimental import pallas as pl
from jax.experimental.pallas import tpu as pltpu
from jax.sharding import PartitionSpec as P

MESH = pl.DeviceIdType.MESH
BF16 = jnp.bfloat16
F32 = jnp.float32
OTHER = 16
NAMES = (
    ["S1", "S2", "L2", "L3", "L4", "G", "A1", "A2"]
    + ["Y1", "Y2", "X1", "X2", "OY1", "OY2", "OX1", "OX2"]
    + ["B2", "B3", "B6", "B7", "R0", "R1", "Q0", "Q1", "CG", "CH"]
    + [f"C{s}" for s in (0, 2, 3, 4, 5, 6, 7)]
    + [f"D{s}" for s in (0, 2, 3, 4, 5, 6, 7)]
)
IDS = {name: number for number, name in enumerate(NAMES)}
TERM = {2: 0, 3: 1, 6: 2, 7: 3, 5: 4, 4: 5}


def kernel(x_ref, w_ref, g_ref, out_ref, ig_ref, dw_ref, xb, sx, wb, gb, rb, sb, acc_o, acc_g, ob, db,
           send_sem, recv_sem, x_sem, g_sem, w_sem, o_sem):
    feat = lax.axis_index("feat")
    dp = lax.axis_index("dp")
    y = feat % 4
    z_lo = (feat // 4) % 4
    x = feat // 16
    side = dp // 2
    core = dp % 2
    z = side * 4 + z_lo
    ey = 1 - 2 * (y % 2)
    ex = 1 - 2 * (x % 2)
    ez = 1 - 2 * (z % 2)
    middle = ((z_lo + 1) // 2) % 2
    end = 1 - middle
    away = 1 - side

    def at_y(step):
        return (x * 16 + z_lo * 4 + (y + step + 4) % 4, dp)

    def at_x(step):
        return (((x + step + 4) % 4) * 16 + z_lo * 4 + y, dp)

    def at_z(step):
        there = (z + step + 8) % 8
        return (x * 16 + (there % 4) * 4 + y, (there // 4) * 2 + core)

    sibling = (feat, side * 2 + 1 - core)
    z_first = at_z(ez)
    z_second = (x * 16 + ((z_lo + 2) % 4) * 4 + y, dp)
    second = end * (OTHER + 5) + middle * (10 + away)

    loads = []
    for d in range(4):
        for r in range(2):
            load = pltpu.make_async_copy(
                x_ref.at[:, pl.ds(r * 512 + d * 128, 128)], xb.at[d // 2, d % 2, r], x_sem.at[d * 2 + r]
            )
            load.start()
            loads.append(load)
    g_loads = []
    for r in range(2):
        load = pltpu.make_async_copy(g_ref.at[:, pl.ds(r * 512, 512)], gb.at[r, 0], g_sem.at[r])
        load.start()
        g_loads.append(load)
    w_loads = {}
    for s in (3, 7, 2, 6, 0, 1, 4, 5):
        w_loads[s] = pltpu.make_async_copy(w_ref.at[:, s], wb.at[s], w_sem.at[s])
        w_loads[s].start()

    barrier = pltpu.get_barrier_semaphore()
    friends = [sibling, at_z(1), at_z(-1), at_z(2), at_z(-2), at_z(4), at_y(1), at_y(-1), at_y(2), at_x(1), at_x(-1), at_x(2)]
    for friend in friends:
        pl.semaphore_signal(barrier, inc=1, device_id=friend, device_id_type=MESH)
    pl.semaphore_wait(barrier, len(friends))

    copies = {}

    def send(name, src, dst, device):
        copies[name] = pltpu.make_async_remote_copy(
            src_ref=src, dst_ref=dst, send_sem=send_sem.at[IDS[name]], recv_sem=recv_sem.at[IDS[name]],
            device_id=device, device_id_type=MESH,
        )
        copies[name].start()

    def arrived(name):
        copies[name].wait_recv()

    def share_same(s):
        send(f"C{s}", xb.at[2 * s + side, 1 - core], sx.at[s, 0], sibling)

    def share_other(s):
        send(f"D{s}", xb.at[OTHER + s, 1 - core], sx.at[s, 1], sibling)

    def forward(s, start=False):
        base = 0 if s == 1 else 2 * s

        def row(r, carry):
            k = 1 - r if s == 1 else r
            block = jnp.concatenate([xb[base + d // 2, d % 2, k] for d in range(4)], axis=1)
            part = jnp.dot(block, wb[s, r], preferred_element_type=F32)
            if start:
                acc_o[r] = part
            else:
                acc_o[r] += part
            return carry

        lax.fori_loop(0, 2, row, 0)

    def term(s, r, q=0):
        return lax.dot_general(gb[r, q], wb[s, r], (((1,), (1,)), ((), ())), preferred_element_type=F32)

    def back(s):
        def row(r, carry):
            sb[TERM[s], r] = term(s, r).astype(BF16)
            return carry

        lax.fori_loop(0, 2, row, 0)

    def back_local():
        def row(r, carry):
            acc_g[r] = term(0, r) + term(1, 1 - r).astype(BF16).astype(F32)
            return carry

        lax.fori_loop(0, 2, row, 0)

    def add_terms(k):
        def row(r, carry):
            acc_g[r] += rb[k, r].astype(F32)
            return carry

        lax.fori_loop(0, 2, row, 0)

    stores = []

    def weight_grad(s):
        base = 0 if s == 1 else s

        def row(r, carry):
            k = 1 - r if s == 1 else r
            tokens = jnp.concatenate(
                [xb[2 * base + side, core, k], sx[base, 0, k], xb[OTHER + base, core, k], sx[base, 1, k]], axis=0
            )
            total = lax.dot_general(
                tokens, gb[r].reshape(1024, 512), (((0,), (0,)), ((), ())), preferred_element_type=F32
            )
            db[s, r] = total.astype(BF16)
            return carry

        lax.fori_loop(0, 2, row, 0)
        store = pltpu.make_async_copy(db.at[s], dw_ref.at[:, s], o_sem.at[4 + s])
        store.start()
        stores.append(store)

    for load in loads:
        load.wait()
    send("S1", xb.at[away], xb.at[8 + away], z_first)
    send("L2", xb.at[away], xb.at[second], at_z(-2 * ez))
    send("Y1", xb.at[pl.ds(0, 2)], xb.at[pl.ds(4, 2)], at_y(ey))
    send("X1", xb.at[pl.ds(0, 2)], xb.at[pl.ds(12, 2)], at_x(ex))
    for load in g_loads:
        load.wait()
    send("G", gb.at[:, 0], gb.at[:, 2], at_z(4))
    share_same(0)
    send("CG", gb.at[:, 0], gb.at[:, 1], sibling)

    for s, device in ((3, at_y(2)), (7, at_x(2)), (2, at_y(ey)), (6, at_x(ex))):
        w_loads[s].wait()
        back(s)
        send(f"B{s}", sb.at[TERM[s]], rb.at[TERM[s]], device)
    w_loads[0].wait()
    w_loads[1].wait()
    forward(0, start=True)
    forward(1)
    back_local()
    w_loads[4].wait()
    w_loads[5].wait()

    arrived("S1")
    send("S2", xb.at[8 + away], xb.at[second], at_z(-ez))
    arrived("L2")
    send("L3", xb.at[middle * (OTHER + 5) + end * (10 + away)], xb.at[OTHER + 4], at_z(-ez))
    arrived("Y1")
    send("Y2", xb.at[pl.ds(4, 2)], xb.at[pl.ds(6, 2)], at_y(-ey))
    share_same(2)
    arrived("X1")
    send("X2", xb.at[pl.ds(12, 2)], xb.at[pl.ds(14, 2)], at_x(-ex))
    share_same(6)
    forward(2)
    forward(6)

    arrived("L3")
    send("L4", xb.at[OTHER + 4], xb.at[OTHER + 0], z_first)
    share_other(4)
    send("A1", xb.at[side], xb.at[8 + side], z_first)
    send("A2", xb.at[side], xb.at[10 + side], z_second)
    arrived("S2")
    share_other(5)
    arrived("Y2")
    share_same(3)
    arrived("X2")
    share_same(7)
    forward(3)
    forward(7)

    arrived("G")
    send("CH", gb.at[:, 2], gb.at[:, 3], sibling)
    for r in range(2):
        sb[TERM[5], r] = term(5, r, 2 * end).astype(BF16)
        send(f"R{r}", sb.at[TERM[5], r], rb.at[TERM[5], r], at_z(-ez))

    arrived("L4")
    send("OY1", xb.at[OTHER + 0], xb.at[OTHER + 2], at_y(ey))
    send("OX1", xb.at[OTHER + 0], xb.at[OTHER + 6], at_x(ex))
    share_other(0)
    for s in (3, 7, 2, 6):
        arrived(f"B{s}")
        add_terms(TERM[s])

    arrived("OY1")
    send("OY2", xb.at[OTHER + 2], xb.at[OTHER + 3], at_y(-ey))
    share_other(2)
    arrived("OX1")
    send("OX2", xb.at[OTHER + 6], xb.at[OTHER + 7], at_x(-ex))
    share_other(6)
    for r in range(2):
        arrived(f"R{r}")
        total = term(4, r).astype(BF16).astype(F32) + rb[TERM[5], r].astype(F32)
        sb[TERM[4], r] = total.astype(BF16)
        send(f"Q{r}", sb.at[TERM[4], r], rb.at[TERM[4], r], z_first)

    for name in ("C0", "CG", "CH", "D0"):
        arrived(name)
    weight_grad(0)
    weight_grad(1)
    for s in (2, 6):
        arrived(f"C{s}")
        arrived(f"D{s}")
        weight_grad(s)
    arrived("OY2")
    share_other(3)
    arrived("OX2")
    share_other(7)
    for s in (3, 7):
        arrived(f"C{s}")
        arrived(f"D{s}")
        weight_grad(s)

    arrived("A1")
    share_same(4)
    forward(4)
    arrived("A2")
    share_same(5)
    forward(5)
    for r in range(2):
        ob[0, r] = acc_o[r].astype(BF16)
        store = pltpu.make_async_copy(ob.at[0, r], out_ref.at[:, pl.ds(r * 512, 512)], o_sem.at[r])
        store.start()
        stores.append(store)
    for s in (4, 5):
        arrived(f"C{s}")
        arrived(f"D{s}")
        weight_grad(s)
    for r in range(2):
        arrived(f"Q{r}")
        ob[1, r] = (acc_g[r] + rb[TERM[4], r].astype(F32)).astype(BF16)
        store = pltpu.make_async_copy(ob.at[1, r], ig_ref.at[:, pl.ds(r * 512, 512)], o_sem.at[2 + r])
        store.start()
        stores.append(store)

    for name in NAMES:
        copies[name].wait_send()
    for store in stores:
        store.wait()


def body(inputs, weights, cotangent):
    n = len(NAMES)
    return pl.pallas_call(
        kernel,
        out_shape=(
            jax.ShapeDtypeStruct((256, 1024), BF16),
            jax.ShapeDtypeStruct((256, 1024), BF16),
            jax.ShapeDtypeStruct((2, 8, 128, 512), BF16),
        ),
        in_specs=[pl.BlockSpec(memory_space=pl.ANY)] * 3,
        out_specs=[pl.BlockSpec(memory_space=pl.ANY)] * 3,
        scratch_shapes=[
            pltpu.VMEM((24, 2, 2, 256, 128), BF16),
            pltpu.VMEM((8, 2, 2, 256, 128), BF16),
            pltpu.VMEM((8, 2, 512, 512), BF16),
            pltpu.VMEM((2, 4, 256, 512), BF16),
            pltpu.VMEM((6, 2, 256, 512), BF16),
            pltpu.VMEM((6, 2, 256, 512), BF16),
            pltpu.VMEM((2, 256, 512), F32),
            pltpu.VMEM((2, 256, 512), F32),
            pltpu.VMEM((2, 2, 256, 512), BF16),
            pltpu.VMEM((8, 2, 128, 512), BF16),
            pltpu.SemaphoreType.DMA((n,)),
            pltpu.SemaphoreType.DMA((n,)),
            pltpu.SemaphoreType.DMA((8,)),
            pltpu.SemaphoreType.DMA((2,)),
            pltpu.SemaphoreType.DMA((8,)),
            pltpu.SemaphoreType.DMA((12,)),
        ],
        compiler_params=pltpu.CompilerParams(
            collective_id=0, has_side_effects=True, vmem_limit_bytes=56 * 2**20
        ),
        cost_estimate=pl.CostEstimate(flops=6442450944, bytes_accessed=12 * 2**20, transcendentals=0),
    )(inputs, weights, cotangent)


def solution(mesh):
    in_specs = (P("dp", "feat"), P("feat", None, None, None), P("dp", "feat"))
    out_specs = (P("dp", "feat"), P("dp", "feat"), P("feat", None, "dp", None))
    return jax.shard_map(body, mesh=mesh, in_specs=in_specs, out_specs=out_specs, check_vma=False)
```

```python
import jax
import jax.numpy as jnp
from jax import lax
from jax.experimental import pallas as pl
from jax.experimental.pallas import tpu as pltpu
from jax.sharding import PartitionSpec as P

MESH = pl.DeviceIdType.MESH
BF16 = jnp.bfloat16
F32 = jnp.float32
OTHER = 16
NAMES = (
    ["GP1", "GM1", "GP2", "GM2", "GP3", "GM3", "GP4", "GM4", "S1", "S2", "L1", "L2", "L3", "L4", "A1P"]
    + ["Y1", "Y2", "X1", "X2", "OY1", "OY2", "OX1", "OX2"]
    + ["B2", "B3", "B6", "B7", "R0", "R1", "Q0", "Q1", "CG", "CH"]
    + [f"C{s}" for s in (0, 2, 3, 4, 5, 6, 7)]
    + [f"D{s}" for s in (0, 2, 3, 4, 5, 6, 7)]
)
MIDDLE = ["A1M", "A2P", "A2M"]
IDS = {name: number for number, name in enumerate(NAMES + MIDDLE)}
TERM = {2: 0, 3: 1, 6: 2, 7: 3, 5: 4, 4: 5}


def kernel(x_ref, w_ref, g_ref, out_ref, ig_ref, dw_ref, xb, sx, wb, gb, gt, at, rb, sb, acc_o, acc_g, ob, db,
           send_sem, recv_sem, x_sem, g_sem, w_sem, o_sem):
    feat = lax.axis_index("feat")
    dp = lax.axis_index("dp")
    y = feat % 4
    z_lo = (feat // 4) % 4
    x = feat // 16
    side = dp // 2
    core = dp % 2
    z = side * 4 + z_lo
    ey = 1 - 2 * (y % 2)
    ex = 1 - 2 * (x % 2)
    ez = 1 - 2 * (z % 2)
    middle = ((z_lo + 1) // 2) % 2
    end = 1 - middle
    away = 1 - side

    def at_y(step):
        return (x * 16 + z_lo * 4 + (y + step + 4) % 4, dp)

    def at_x(step):
        return (((x + step + 4) % 4) * 16 + z_lo * 4 + y, dp)

    def at_z(step):
        there = (z + step + 8) % 8
        return (x * 16 + (there % 4) * 4 + y, (there // 4) * 2 + core)

    sibling = (feat, side * 2 + 1 - core)
    z_first = at_z(ez)
    z_last = at_z(-ez)
    odd = z % 2
    even = 1 - odd
    second = end * (OTHER + 5) + middle * (10 + away)
    mine = middle * (OTHER + 5) + end * (10 + away)

    loads = []
    for d in range(4):
        for r in range(2):
            load = pltpu.make_async_copy(
                x_ref.at[:, pl.ds(r * 512 + d * 128, 128)], xb.at[d // 2, d % 2, r], x_sem.at[d * 2 + r]
            )
            load.start()
            loads.append(load)
    g_loads = []
    for r in range(2):
        load = pltpu.make_async_copy(g_ref.at[:, pl.ds(r * 512, 512)], gb.at[r, 0], g_sem.at[r])
        load.start()
        g_loads.append(load)
    w_loads = {}
    for s in (3, 7, 2, 6, 0, 1, 4, 5):
        w_loads[s] = pltpu.make_async_copy(w_ref.at[:, s], wb.at[s], w_sem.at[s])
        w_loads[s].start()

    barrier = pltpu.get_barrier_semaphore()
    friends = [sibling, at_z(1), at_z(-1), at_y(1), at_y(-1), at_y(2), at_x(1), at_x(-1), at_x(2)]
    for friend in friends:
        pl.semaphore_signal(barrier, inc=1, device_id=friend, device_id_type=MESH)
    pl.semaphore_wait(barrier, len(friends))

    routes = {}

    def descriptor(name):
        src, dst, device = routes[name]
        return pltpu.make_async_remote_copy(
            src_ref=src, dst_ref=dst, send_sem=send_sem.at[IDS[name]], recv_sem=recv_sem.at[IDS[name]],
            device_id=device, device_id_type=MESH,
        )

    def send(name, src, dst, device):
        routes[name] = (src, dst, device)
        descriptor(name).start()

    def arrived(name):
        descriptor(name).wait_recv()

    def share_same(s):
        send(f"C{s}", xb.at[2 * s + side, 1 - core], sx.at[s, 0], sibling)

    def share_other(s):
        send(f"D{s}", xb.at[OTHER + s, 1 - core], sx.at[s, 1], sibling)

    def forward(s, start=False):
        base = 0 if s == 1 else 2 * s

        def row(r, carry):
            k = 1 - r if s == 1 else r
            block = jnp.concatenate([xb[base + d // 2, d % 2, k] for d in range(4)], axis=1)
            part = jnp.dot(block, wb[s, r], preferred_element_type=F32)
            if start:
                acc_o[r] = part
            else:
                acc_o[r] += part
            return carry

        lax.fori_loop(0, 2, row, 0)

    def term(s, r, q=0):
        return lax.dot_general(gb[r, q], wb[s, r], (((1,), (1,)), ((), ())), preferred_element_type=F32)

    def back(s):
        def row(r, carry):
            sb[TERM[s], r] = term(s, r).astype(BF16)
            return carry

        lax.fori_loop(0, 2, row, 0)

    def back_local():
        def row(r, carry):
            acc_g[r] = term(0, r) + term(1, 1 - r).astype(BF16).astype(F32)
            return carry

        lax.fori_loop(0, 2, row, 0)

    def add_terms(k):
        def row(r, carry):
            acc_g[r] += rb[k, r].astype(F32)
            return carry

        lax.fori_loop(0, 2, row, 0)

    for r in range(2):
        routes[f"R{r}"] = (sb.at[TERM[5], r], rb.at[TERM[5], r], z_last)
        routes[f"Q{r}"] = (sb.at[TERM[4], r], rb.at[TERM[4], r], z_first)

    def relay(r, q):
        sb[TERM[5], r] = term(5, r, q).astype(BF16)
        descriptor(f"R{r}").start()

    def add_and_pass(r):
        arrived(f"R{r}")
        total = term(4, r).astype(BF16).astype(F32) + rb[TERM[5], r].astype(F32)
        sb[TERM[4], r] = total.astype(BF16)
        descriptor(f"Q{r}").start()

    stores = []

    def weight_grad(s):
        base = 0 if s == 1 else s

        def row(r, carry):
            k = 1 - r if s == 1 else r
            tokens = jnp.concatenate(
                [xb[2 * base + side, core, k], sx[base, 0, k], xb[OTHER + base, core, k], sx[base, 1, k]], axis=0
            )
            total = lax.dot_general(
                tokens, gb[r].reshape(1024, 512), (((0,), (0,)), ((), ())), preferred_element_type=F32
            )
            db[s, r] = total.astype(BF16)
            return carry

        lax.fori_loop(0, 2, row, 0)
        store = pltpu.make_async_copy(db.at[s], dw_ref.at[:, s], o_sem.at[4 + s])
        store.start()
        stores.append(store)

    routes["A1M"] = (xb.at[side], at.at[1], z_last)
    routes["A2P"] = (at.at[1], xb.at[10 + side], z_first)
    routes["A2M"] = (xb.at[8 + side], xb.at[10 + side], z_last)

    for load in g_loads:
        load.wait()
    send("GP1", gb.at[odd, 0], gt.at[0, 0], z_first)
    send("GM1", gb.at[even, 0], gt.at[1, 0], z_last)
    for load in loads:
        load.wait()
    send("S1", xb.at[away], xb.at[8 + away], z_first)
    send("L1", xb.at[away], at.at[0], z_last)
    send("Y1", xb.at[pl.ds(0, 2)], xb.at[pl.ds(4, 2)], at_y(ey))
    send("X1", xb.at[pl.ds(0, 2)], xb.at[pl.ds(12, 2)], at_x(ex))
    share_same(0)
    send("CG", gb.at[:, 0], gb.at[:, 1], sibling)

    for s, device in ((3, at_y(2)), (7, at_x(2)), (2, at_y(ey)), (6, at_x(ex))):
        w_loads[s].wait()
        back(s)
        send(f"B{s}", sb.at[TERM[s]], rb.at[TERM[s]], device)
    for s in (5, 4, 0, 1):
        w_loads[s].wait()

    arrived("GP1")
    send("GM2", gt.at[0, 0], gt.at[1, 1], z_last)
    arrived("GM1")
    send("GP2", gt.at[1, 0], gt.at[0, 1], z_first)
    forward(0, start=True)
    forward(1)
    arrived("S1")
    send("S2", xb.at[8 + away], xb.at[second], z_last)
    arrived("L1")
    send("L2", at.at[0], xb.at[second], z_first)
    back_local()
    arrived("Y1")
    send("Y2", xb.at[pl.ds(4, 2)], xb.at[pl.ds(6, 2)], at_y(-ey))
    share_same(2)
    arrived("X1")
    send("X2", xb.at[pl.ds(12, 2)], xb.at[pl.ds(14, 2)], at_x(-ex))
    share_same(6)

    arrived("GP2")
    send("GM3", gt.at[0, 1], gt.at[1, 2], z_last)
    arrived("GM2")
    send("GP3", gt.at[1, 1], gt.at[0, 2], z_first)
    send("A1P", xb.at[side], xb.at[8 + side], z_first)
    forward(2)
    forward(6)
    arrived("L2")
    send("L3", xb.at[mine], xb.at[OTHER + 4], z_last)
    arrived("S2")
    share_other(5)
    arrived("Y2")
    share_same(3)
    arrived("X2")
    share_same(7)

    arrived("GP3")
    send("GM4", gt.at[0, 2], gb.at[even, 2], z_last)
    arrived("GM3")
    send("GP4", gt.at[1, 2], gb.at[odd, 2], z_first)
    forward(3)
    forward(7)
    arrived("L3")
    send("L4", xb.at[OTHER + 4], xb.at[OTHER + 0], z_first)
    share_other(4)

    @pl.when(middle == 1)
    def _():
        descriptor("A1M").start()
        relay(0, 0)
        relay(1, 0)

    arrived("A1P")

    @pl.when(middle == 1)
    def _():
        descriptor("A2M").start()

    share_same(4)
    arrived("GP4")
    arrived("GM4")

    @pl.when(end == 1)
    def _():
        relay(0, 2)
        relay(1, 2)

    send("CH", gb.at[:, 2], gb.at[:, 3], sibling)
    forward(4)
    for s in (3, 7, 2, 6):
        arrived(f"B{s}")
        add_terms(TERM[s])

    arrived("L4")
    send("OY1", xb.at[OTHER + 0], xb.at[OTHER + 2], at_y(ey))
    send("OX1", xb.at[OTHER + 0], xb.at[OTHER + 6], at_x(ex))
    share_other(0)

    @pl.when(middle == 1)
    def _():
        arrived("A1M")
        descriptor("A2P").start()

    add_and_pass(0)
    for name in ("C0", "CG", "CH", "D0"):
        arrived(name)
    weight_grad(0)
    arrived("OY1")
    send("OY2", xb.at[OTHER + 2], xb.at[OTHER + 3], at_y(-ey))
    share_other(2)
    arrived("OX1")
    send("OX2", xb.at[OTHER + 6], xb.at[OTHER + 7], at_x(-ex))
    share_other(6)
    add_and_pass(1)
    weight_grad(1)
    for s in (4, 2, 6):
        arrived(f"C{s}")
        arrived(f"D{s}")
        weight_grad(s)
    arrived("OY2")
    share_other(3)
    arrived("OX2")
    share_other(7)

    @pl.when(end == 1)
    def _():
        arrived("A2P")

    @pl.when(middle == 1)
    def _():
        arrived("A2M")

    share_same(5)
    forward(5)
    for r in range(2):
        ob[0, r] = acc_o[r].astype(BF16)
        store = pltpu.make_async_copy(ob.at[0, r], out_ref.at[:, pl.ds(r * 512, 512)], o_sem.at[r])
        store.start()
        stores.append(store)
    for s in (3, 7, 5):
        arrived(f"C{s}")
        arrived(f"D{s}")
        weight_grad(s)
    for r in range(2):
        arrived(f"Q{r}")
        ob[1, r] = (acc_g[r] + rb[TERM[4], r].astype(F32)).astype(BF16)
        store = pltpu.make_async_copy(ob.at[1, r], ig_ref.at[:, pl.ds(r * 512, 512)], o_sem.at[2 + r])
        store.start()
        stores.append(store)

    for name in NAMES:
        descriptor(name).wait_send()

    @pl.when(middle == 1)
    def _():
        for name in MIDDLE:
            descriptor(name).wait_send()

    for store in stores:
        store.wait()


def body(inputs, weights, cotangent):
    n = len(NAMES + MIDDLE)
    return pl.pallas_call(
        kernel,
        out_shape=(
            jax.ShapeDtypeStruct((256, 1024), BF16),
            jax.ShapeDtypeStruct((256, 1024), BF16),
            jax.ShapeDtypeStruct((2, 8, 128, 512), BF16),
        ),
        in_specs=[pl.BlockSpec(memory_space=pl.ANY)] * 3,
        out_specs=[pl.BlockSpec(memory_space=pl.ANY)] * 3,
        scratch_shapes=[
            pltpu.VMEM((24, 2, 2, 256, 128), BF16),
            pltpu.VMEM((8, 2, 2, 256, 128), BF16),
            pltpu.VMEM((8, 2, 512, 512), BF16),
            pltpu.VMEM((2, 4, 256, 512), BF16),
            pltpu.VMEM((2, 3, 256, 512), BF16),
            pltpu.VMEM((2, 2, 2, 256, 128), BF16),
            pltpu.VMEM((6, 2, 256, 512), BF16),
            pltpu.VMEM((6, 2, 256, 512), BF16),
            pltpu.VMEM((2, 256, 512), F32),
            pltpu.VMEM((2, 256, 512), F32),
            pltpu.VMEM((2, 2, 256, 512), BF16),
            pltpu.VMEM((8, 2, 128, 512), BF16),
            pltpu.SemaphoreType.DMA((n,)),
            pltpu.SemaphoreType.DMA((n,)),
            pltpu.SemaphoreType.DMA((8,)),
            pltpu.SemaphoreType.DMA((2,)),
            pltpu.SemaphoreType.DMA((8,)),
            pltpu.SemaphoreType.DMA((12,)),
        ],
        compiler_params=pltpu.CompilerParams(
            collective_id=0, has_side_effects=True, vmem_limit_bytes=56 * 2**20
        ),
        cost_estimate=pl.CostEstimate(flops=6442450944, bytes_accessed=12 * 2**20, transcendentals=0),
    )(inputs, weights, cotangent)


def solution(mesh):
    in_specs = (P("dp", "feat"), P("feat", None, None, None), P("dp", "feat"))
    out_specs = (P("dp", "feat"), P("dp", "feat"), P("feat", None, "dp", None))
    return jax.shard_map(body, mesh=mesh, in_specs=in_specs, out_specs=out_specs, check_vma=False)
```

```python
import jax
import jax.numpy as jnp
from jax import lax
from jax.experimental import pallas as pl
from jax.experimental.pallas import tpu as pltpu
from jax.sharding import PartitionSpec as P

MESH = pl.DeviceIdType.MESH
BF16 = jnp.bfloat16
F32 = jnp.float32
OTHER = 16
NAMES = (
    ["GP1", "GM1", "GP2", "GM2", "GP3", "GM3", "GP4", "GM4", "S1", "S2", "L1", "L2", "L3", "L4", "A1P"]
    + ["Y1", "Y2", "X1", "X2", "OY1", "OY2", "OX1", "OX2"]
    + ["B2", "B3", "B6", "B7", "R0", "R1", "Q0", "Q1", "CG", "CH"]
    + [f"C{s}" for s in (0, 2, 3, 4, 5, 6, 7)]
    + [f"D{s}" for s in (0, 2, 3, 4, 5, 6, 7)]
)
MIDDLE = ["A1M", "A2P", "A2M"]
IDS = {name: number for number, name in enumerate(NAMES + MIDDLE)}
TERM = {2: 0, 3: 1, 6: 2, 7: 3, 5: 4, 4: 5}


def kernel(x_ref, w_ref, g_ref, out_ref, ig_ref, dw_ref, xb, sx, wb, gb, gt, at, rb, sb, acc_o, acc_g,
           send_sem, recv_sem, x_sem, g_sem, w_sem):
    feat = lax.axis_index("feat")
    dp = lax.axis_index("dp")
    y = feat % 4
    z_lo = (feat // 4) % 4
    x = feat // 16
    side = dp // 2
    core = dp % 2
    z = side * 4 + z_lo
    ey = 1 - 2 * (y % 2)
    ex = 1 - 2 * (x % 2)
    ez = 1 - 2 * (z % 2)
    middle = ((z_lo + 1) // 2) % 2
    end = 1 - middle
    away = 1 - side

    def at_y(step):
        return (x * 16 + z_lo * 4 + (y + step + 4) % 4, dp)

    def at_x(step):
        return (((x + step + 4) % 4) * 16 + z_lo * 4 + y, dp)

    def at_z(step):
        there = (z + step + 8) % 8
        return (x * 16 + (there % 4) * 4 + y, (there // 4) * 2 + core)

    sibling = (feat, side * 2 + 1 - core)
    z_first = at_z(ez)
    z_last = at_z(-ez)
    odd = z % 2
    even = 1 - odd
    second = end * (OTHER + 5) + middle * (10 + away)
    mine = middle * (OTHER + 5) + end * (10 + away)

    loads = []
    for d in range(4):
        for r in range(2):
            load = pltpu.make_async_copy(
                x_ref.at[:, pl.ds(r * 512 + d * 128, 128)], xb.at[d // 2, d % 2, r], x_sem.at[d * 2 + r]
            )
            load.start()
            loads.append(load)
    g_loads = []
    for r in range(2):
        load = pltpu.make_async_copy(g_ref.at[:, pl.ds(r * 512, 512)], gb.at[r, 0], g_sem.at[r])
        load.start()
        g_loads.append(load)
    w_loads = {}
    for s in (3, 7, 2, 6, 0, 1, 4, 5):
        w_loads[s] = pltpu.make_async_copy(w_ref.at[:, s], wb.at[s], w_sem.at[s])
        w_loads[s].start()

    barrier = pltpu.get_barrier_semaphore()
    friends = [sibling, at_z(1), at_z(-1), at_y(1), at_y(-1), at_y(2), at_x(1), at_x(-1), at_x(2)]
    for friend in friends:
        pl.semaphore_signal(barrier, inc=1, device_id=friend, device_id_type=MESH)
    pl.semaphore_wait(barrier, len(friends))

    routes = {}

    def descriptor(name):
        src, dst, device = routes[name]
        return pltpu.make_async_remote_copy(
            src_ref=src, dst_ref=dst, send_sem=send_sem.at[IDS[name]], recv_sem=recv_sem.at[IDS[name]],
            device_id=device, device_id_type=MESH,
        )

    def send(name, src, dst, device):
        routes[name] = (src, dst, device)
        descriptor(name).start()

    def arrived(name):
        descriptor(name).wait_recv()

    def share_same(s):
        send(f"C{s}", xb.at[2 * s + side, 1 - core], sx.at[s, 0], sibling)

    def share_other(s):
        send(f"D{s}", xb.at[OTHER + s, 1 - core], sx.at[s, 1], sibling)

    def forward(s, start=False):
        base = 0 if s == 1 else 2 * s

        def row(r, carry):
            k = 1 - r if s == 1 else r
            block = jnp.concatenate([xb[base + d // 2, d % 2, k] for d in range(4)], axis=1)
            part = jnp.dot(block, wb[s, r], preferred_element_type=F32)
            if start:
                acc_o[r] = part
            else:
                acc_o[r] += part
            return carry

        lax.fori_loop(0, 2, row, 0)

    def term(s, r, q=0):
        return lax.dot_general(gb[r, q], wb[s, r], (((1,), (1,)), ((), ())), preferred_element_type=F32)

    def back(s):
        def row(r, carry):
            sb[TERM[s], r] = term(s, r).astype(BF16)
            return carry

        lax.fori_loop(0, 2, row, 0)

    def back_local():
        def row(r, carry):
            acc_g[r] = term(0, r) + term(1, 1 - r).astype(BF16).astype(F32)
            return carry

        lax.fori_loop(0, 2, row, 0)

    def add_terms(k):
        def row(r, carry):
            acc_g[r] += rb[k, r].astype(F32)
            return carry

        lax.fori_loop(0, 2, row, 0)

    for r in range(2):
        routes[f"R{r}"] = (sb.at[TERM[5], r], rb.at[TERM[5], r], z_last)
        routes[f"Q{r}"] = (sb.at[TERM[4], r], rb.at[TERM[4], r], z_first)

    def relay(r, q):
        sb[TERM[5], r] = term(5, r, q).astype(BF16)
        descriptor(f"R{r}").start()

    def add_and_pass(r):
        arrived(f"R{r}")
        total = term(4, r).astype(BF16).astype(F32) + rb[TERM[5], r].astype(F32)
        sb[TERM[4], r] = total.astype(BF16)
        descriptor(f"Q{r}").start()

    def weight_grad(s):
        base = 0 if s == 1 else s

        def row(r, carry):
            k = 1 - r if s == 1 else r
            tokens = jnp.concatenate(
                [xb[2 * base + side, core, k], sx[base, 0, k], xb[OTHER + base, core, k], sx[base, 1, k]], axis=0
            )
            total = lax.dot_general(
                tokens, gb[r].reshape(1024, 512), (((0,), (0,)), ((), ())), preferred_element_type=F32
            )
            dw_ref[r, s] = total.astype(BF16)
            return carry

        lax.fori_loop(0, 2, row, 0)

    routes["A1M"] = (xb.at[side], at.at[1], z_last)
    routes["A2P"] = (at.at[1], xb.at[10 + side], z_first)
    routes["A2M"] = (xb.at[8 + side], xb.at[10 + side], z_last)

    for load in g_loads:
        load.wait()
    send("GP1", gb.at[odd, 0], gt.at[0, 0], z_first)
    send("GM1", gb.at[even, 0], gt.at[1, 0], z_last)
    for load in loads:
        load.wait()
    send("S1", xb.at[away], xb.at[8 + away], z_first)
    send("L1", xb.at[away], at.at[0], z_last)
    send("Y1", xb.at[pl.ds(0, 2)], xb.at[pl.ds(4, 2)], at_y(ey))
    send("X1", xb.at[pl.ds(0, 2)], xb.at[pl.ds(12, 2)], at_x(ex))
    share_same(0)
    send("CG", gb.at[:, 0], gb.at[:, 1], sibling)

    for s, device in ((3, at_y(2)), (7, at_x(2)), (2, at_y(ey)), (6, at_x(ex))):
        w_loads[s].wait()
        back(s)
        send(f"B{s}", sb.at[TERM[s]], rb.at[TERM[s]], device)
    for s in (5, 4, 0, 1):
        w_loads[s].wait()

    arrived("GP1")
    send("GM2", gt.at[0, 0], gt.at[1, 1], z_last)
    arrived("GM1")
    send("GP2", gt.at[1, 0], gt.at[0, 1], z_first)
    forward(0, start=True)
    forward(1)
    arrived("S1")
    send("S2", xb.at[8 + away], xb.at[second], z_last)
    arrived("L1")
    send("L2", at.at[0], xb.at[second], z_first)
    back_local()
    arrived("Y1")
    send("Y2", xb.at[pl.ds(4, 2)], xb.at[pl.ds(6, 2)], at_y(-ey))
    share_same(2)
    arrived("X1")
    send("X2", xb.at[pl.ds(12, 2)], xb.at[pl.ds(14, 2)], at_x(-ex))
    share_same(6)

    arrived("GP2")
    send("GM3", gt.at[0, 1], gt.at[1, 2], z_last)
    arrived("GM2")
    send("GP3", gt.at[1, 1], gt.at[0, 2], z_first)
    send("A1P", xb.at[side], xb.at[8 + side], z_first)
    forward(2)
    forward(6)
    arrived("L2")
    send("L3", xb.at[mine], xb.at[OTHER + 4], z_last)
    arrived("S2")
    share_other(5)
    arrived("Y2")
    share_same(3)
    arrived("X2")
    share_same(7)

    arrived("GP3")
    send("GM4", gt.at[0, 2], gb.at[even, 2], z_last)
    arrived("GM3")
    send("GP4", gt.at[1, 2], gb.at[odd, 2], z_first)
    forward(3)
    forward(7)
    arrived("L3")
    send("L4", xb.at[OTHER + 4], xb.at[OTHER + 0], z_first)
    share_other(4)

    @pl.when(middle == 1)
    def _():
        descriptor("A1M").start()
        relay(0, 0)
        relay(1, 0)

    arrived("A1P")

    @pl.when(middle == 1)
    def _():
        descriptor("A2M").start()

    share_same(4)
    arrived("GP4")
    arrived("GM4")

    @pl.when(end == 1)
    def _():
        relay(0, 2)
        relay(1, 2)

    send("CH", gb.at[:, 2], gb.at[:, 3], sibling)
    forward(4)
    for s in (3, 7, 2, 6):
        arrived(f"B{s}")
        add_terms(TERM[s])

    arrived("L4")
    send("OY1", xb.at[OTHER + 0], xb.at[OTHER + 2], at_y(ey))
    send("OX1", xb.at[OTHER + 0], xb.at[OTHER + 6], at_x(ex))
    share_other(0)

    @pl.when(middle == 1)
    def _():
        arrived("A1M")
        descriptor("A2P").start()

    add_and_pass(0)
    for name in ("C0", "CG", "CH", "D0"):
        arrived(name)
    weight_grad(0)
    arrived("OY1")
    send("OY2", xb.at[OTHER + 2], xb.at[OTHER + 3], at_y(-ey))
    share_other(2)
    arrived("OX1")
    send("OX2", xb.at[OTHER + 6], xb.at[OTHER + 7], at_x(-ex))
    share_other(6)
    add_and_pass(1)
    weight_grad(1)
    for s in (4, 2, 6):
        arrived(f"C{s}")
        arrived(f"D{s}")
        weight_grad(s)
    arrived("OY2")
    share_other(3)
    arrived("OX2")
    share_other(7)

    @pl.when(end == 1)
    def _():
        arrived("A2P")

    @pl.when(middle == 1)
    def _():
        arrived("A2M")

    share_same(5)
    forward(5)
    for r in range(2):
        out_ref[:, pl.ds(r * 512, 512)] = acc_o[r].astype(BF16)
    for s in (3, 7, 5):
        arrived(f"C{s}")
        arrived(f"D{s}")
        weight_grad(s)
    for r in range(2):
        arrived(f"Q{r}")
        ig_ref[:, pl.ds(r * 512, 512)] = (acc_g[r] + rb[TERM[4], r].astype(F32)).astype(BF16)

    for name in NAMES:
        descriptor(name).wait_send()

    @pl.when(middle == 1)
    def _():
        for name in MIDDLE:
            descriptor(name).wait_send()


def settle(out_in, ig_in, dw_in, out_ref, ig_ref, dw_ref, sem):
    moves = []
    for r in range(2):
        for s in range(0, 8, 4):
            slots = pl.ds(s, 4)
            moves.append((dw_in.at[r, slots], dw_ref.at[r, slots]))
        rows = pl.ds(r * 128, 128)
        moves.append((out_in.at[rows], out_ref.at[rows]))
        moves.append((ig_in.at[rows], ig_ref.at[rows]))
    moves = [pltpu.make_async_copy(src, dst, sem.at[k]) for k, (src, dst) in enumerate(moves)]
    for move in moves:
        move.start()
    for move in moves:
        move.wait()


def body(inputs, weights, cotangent):
    n = len(NAMES + MIDDLE)
    results = pl.pallas_call(
        kernel,
        out_shape=(
            pltpu.VMEM((256, 1024), BF16),
            pltpu.VMEM((256, 1024), BF16),
            pltpu.VMEM((2, 8, 128, 512), BF16),
        ),
        in_specs=[pl.BlockSpec(memory_space=pl.ANY)] * 3,
        out_specs=[pl.BlockSpec(memory_space=pltpu.VMEM)] * 3,
        scratch_shapes=[
            pltpu.VMEM((24, 2, 2, 256, 128), BF16),
            pltpu.VMEM((8, 2, 2, 256, 128), BF16),
            pltpu.VMEM((8, 2, 512, 512), BF16),
            pltpu.VMEM((2, 4, 256, 512), BF16),
            pltpu.VMEM((2, 3, 256, 512), BF16),
            pltpu.VMEM((2, 2, 2, 256, 128), BF16),
            pltpu.VMEM((6, 2, 256, 512), BF16),
            pltpu.VMEM((6, 2, 256, 512), BF16),
            pltpu.VMEM((2, 256, 512), F32),
            pltpu.VMEM((2, 256, 512), F32),
            pltpu.SemaphoreType.DMA((n,)),
            pltpu.SemaphoreType.DMA((n,)),
            pltpu.SemaphoreType.DMA((8,)),
            pltpu.SemaphoreType.DMA((2,)),
            pltpu.SemaphoreType.DMA((8,)),
        ],
        compiler_params=pltpu.CompilerParams(
            collective_id=0, has_side_effects=True, vmem_limit_bytes=56 * 2**20
        ),
        cost_estimate=pl.CostEstimate(flops=6442450944, bytes_accessed=12 * 2**20, transcendentals=0),
    )(inputs, weights, cotangent)
    return pl.pallas_call(
        settle,
        out_shape=tuple(jax.ShapeDtypeStruct(result.shape, result.dtype) for result in results),
        in_specs=[pl.BlockSpec(memory_space=pl.ANY)] * 3,
        out_specs=[pl.BlockSpec(memory_space=pl.ANY)] * 3,
        scratch_shapes=[pltpu.SemaphoreType.DMA((8,))],
        compiler_params=pltpu.CompilerParams(vmem_limit_bytes=8 * 2**20),
    )(*results)


def solution(mesh):
    in_specs = (P("dp", "feat"), P("feat", None, None, None), P("dp", "feat"))
    out_specs = (P("dp", "feat"), P("dp", "feat"), P("feat", None, "dp", None))
    return jax.shard_map(body, mesh=mesh, in_specs=in_specs, out_specs=out_specs, check_vma=False)
```

```python
import jax
import jax.numpy as jnp
from jax import lax
from jax.experimental import pallas as pl
from jax.experimental.pallas import tpu as pltpu
from jax.sharding import PartitionSpec as P

MESH = pl.DeviceIdType.MESH
BF16 = jnp.bfloat16
F32 = jnp.float32
OTHER = 16
NAMES = (
    ["GP1", "GM1", "GP2", "GM2", "GP3", "GM3", "GP4", "GM4", "S1", "S2", "L1", "L2", "L3", "L4", "A1P"]
    + ["Y1", "Y2", "X1", "X2", "OY1", "OY2", "OX1", "OX2"]
    + ["B2", "B3", "B6", "B7", "R0", "R1", "R2", "R3", "Q0", "Q1", "Q2", "Q3", "CG", "CH"]
    + [f"C{s}" for s in (0, 2, 3, 4, 5, 6, 7)]
    + [f"D{s}" for s in (0, 2, 3, 4, 5, 6, 7)]
)
MIDDLE = ["A1M", "A2P", "A2M"]
IDS = {name: number for number, name in enumerate(NAMES + MIDDLE)}
TERM = {2: 0, 3: 1, 6: 2, 7: 3, 5: 4, 4: 5}


def kernel(x_ref, w_ref, g_ref, out_ref, ig_ref, dw_ref, xb, sx, wb, gb, gt, at, rb, sb, acc_o, acc_g,
           send_sem, recv_sem, x_sem, g_sem, w_sem):
    feat = lax.axis_index("feat")
    dp = lax.axis_index("dp")
    y = feat % 4
    z_lo = (feat // 4) % 4
    x = feat // 16
    side = dp // 2
    core = dp % 2
    z = side * 4 + z_lo
    ey = 1 - 2 * (y % 2)
    ex = 1 - 2 * (x % 2)
    ez = 1 - 2 * (z % 2)
    middle = ((z_lo + 1) // 2) % 2
    end = 1 - middle
    away = 1 - side

    def at_y(step):
        return (x * 16 + z_lo * 4 + (y + step + 4) % 4, dp)

    def at_x(step):
        return (((x + step + 4) % 4) * 16 + z_lo * 4 + y, dp)

    def at_z(step):
        there = (z + step + 8) % 8
        return (x * 16 + (there % 4) * 4 + y, (there // 4) * 2 + core)

    sibling = (feat, side * 2 + 1 - core)
    z_first = at_z(ez)
    z_last = at_z(-ez)
    odd = z % 2
    even = 1 - odd
    second = end * (OTHER + 5) + middle * (10 + away)
    mine = middle * (OTHER + 5) + end * (10 + away)

    barrier = pltpu.get_barrier_semaphore()
    friends = [sibling, at_z(1), at_z(-1), at_y(1), at_y(-1), at_y(2), at_x(1), at_x(-1), at_x(2)]
    for friend in friends:
        pl.semaphore_signal(barrier, inc=1, device_id=friend, device_id_type=MESH)
    g_loads = []
    for r in range(2):
        load = pltpu.make_async_copy(g_ref.at[:, pl.ds(r * 512, 512)], gb.at[r, 0], g_sem.at[r])
        load.start()
        g_loads.append(load)
    loads = []
    for d in range(4):
        for r in range(2):
            load = pltpu.make_async_copy(
                x_ref.at[:, pl.ds(r * 512 + d * 128, 128)], xb.at[d // 2, d % 2, r], x_sem.at[d * 2 + r]
            )
            load.start()
            loads.append(load)
    pl.semaphore_wait(barrier, len(friends))

    routes = {}

    def descriptor(name):
        src, dst, device = routes[name]
        return pltpu.make_async_remote_copy(
            src_ref=src, dst_ref=dst, send_sem=send_sem.at[IDS[name]], recv_sem=recv_sem.at[IDS[name]],
            device_id=device, device_id_type=MESH,
        )

    def send(name, src, dst, device):
        routes[name] = (src, dst, device)
        descriptor(name).start()

    def arrived(name):
        descriptor(name).wait_recv()

    def share_same(s):
        send(f"C{s}", xb.at[2 * s + side, 1 - core], sx.at[s, 0], sibling)

    def share_other(s):
        send(f"D{s}", xb.at[OTHER + s, 1 - core], sx.at[s, 1], sibling)

    def forward(s, start=False):
        base = 0 if s == 1 else 2 * s

        def row(r, carry):
            k = 1 - r if s == 1 else r
            block = jnp.concatenate([xb[base + d // 2, d % 2, k] for d in range(4)], axis=1)
            part = jnp.dot(block, wb[s, r], preferred_element_type=F32)
            if start:
                acc_o[r] = part
            else:
                acc_o[r] += part
            return carry

        lax.fori_loop(0, 2, row, 0)

    def term(s, r, q=0):
        return lax.dot_general(gb[r, q], wb[s, r], (((1,), (1,)), ((), ())), preferred_element_type=F32)

    def back(s):
        def row(r, carry):
            sb[TERM[s], r] = term(s, r).astype(BF16)
            return carry

        lax.fori_loop(0, 2, row, 0)

    def back_local():
        def row(r, carry):
            acc_g[r] = term(0, r) + term(1, 1 - r).astype(BF16).astype(F32)
            return carry

        lax.fori_loop(0, 2, row, 0)

    def add_terms(k):
        def row(r, carry):
            acc_g[r] += rb[k, r].astype(F32)
            return carry

        lax.fori_loop(0, 2, row, 0)

    for r in range(2):
        for h in range(2):
            rows = pl.ds(h * 128, 128)
            routes[f"R{2 * r + h}"] = (sb.at[TERM[5], r, rows], rb.at[TERM[5], r, rows], z_last)
            routes[f"Q{2 * r + h}"] = (sb.at[TERM[4], r, rows], rb.at[TERM[4], r, rows], z_first)

    def relay(r, q):
        sb[TERM[5], r] = term(5, r, q).astype(BF16)
        for h in range(2):
            descriptor(f"R{2 * r + h}").start()

    def add_and_pass(r):
        for h in range(2):
            rows = pl.ds(h * 128, 128)
            arrived(f"R{2 * r + h}")
            total = sb[TERM[4], r, rows].astype(F32) + rb[TERM[5], r, rows].astype(F32)
            sb[TERM[4], r, rows] = total.astype(BF16)
            descriptor(f"Q{2 * r + h}").start()

    def weight_grad(s):
        base = 0 if s == 1 else s

        def row(r, carry):
            k = 1 - r if s == 1 else r
            tokens = jnp.concatenate(
                [xb[2 * base + side, core, k], sx[base, 0, k], xb[OTHER + base, core, k], sx[base, 1, k]], axis=0
            )
            total = lax.dot_general(
                tokens, gb[r].reshape(1024, 512), (((0,), (0,)), ((), ())), preferred_element_type=F32
            )
            dw_ref[r, s] = total.astype(BF16)
            return carry

        lax.fori_loop(0, 2, row, 0)

    routes["CH"] = (gb.at[:, 2], gb.at[:, 3], sibling)
    routes["A1M"] = (xb.at[side], at.at[1], z_last)
    routes["A2P"] = (at.at[1], xb.at[10 + side], z_first)
    routes["A2M"] = (xb.at[8 + side], xb.at[10 + side], z_last)

    for load in g_loads:
        load.wait()
    send("GP1", gb.at[odd, 0], gt.at[0, 0], z_first)
    send("GM1", gb.at[even, 0], gt.at[1, 0], z_last)
    for load in loads:
        load.wait()
    send("S1", xb.at[away], xb.at[8 + away], z_first)
    send("L1", xb.at[away], at.at[0], z_last)
    send("Y1", xb.at[pl.ds(0, 2)], xb.at[pl.ds(4, 2)], at_y(ey))
    send("X1", xb.at[pl.ds(0, 2)], xb.at[pl.ds(12, 2)], at_x(ex))
    share_same(0)
    send("CG", gb.at[:, 0], gb.at[:, 1], sibling)
    w_loads = {}
    for s in (3, 7, 2, 6, 0, 1, 4, 5):
        w_loads[s] = pltpu.make_async_copy(w_ref.at[:, s], wb.at[s], w_sem.at[s])
        w_loads[s].start()

    for s, device in ((3, at_y(2)), (7, at_x(2)), (2, at_y(ey)), (6, at_x(ex))):
        w_loads[s].wait()
        back(s)
        send(f"B{s}", sb.at[TERM[s]], rb.at[TERM[s]], device)
    for s in (5, 4, 0, 1):
        w_loads[s].wait()

    arrived("GP1")
    send("GM2", gt.at[0, 0], gt.at[1, 1], z_last)
    arrived("GM1")
    send("GP2", gt.at[1, 0], gt.at[0, 1], z_first)
    forward(0, start=True)
    forward(1)
    arrived("S1")
    send("S2", xb.at[8 + away], xb.at[second], z_last)
    arrived("L1")
    send("L2", at.at[0], xb.at[second], z_first)
    back_local()
    back(4)
    arrived("Y1")
    send("Y2", xb.at[pl.ds(4, 2)], xb.at[pl.ds(6, 2)], at_y(-ey))
    share_same(2)
    arrived("X1")
    send("X2", xb.at[pl.ds(12, 2)], xb.at[pl.ds(14, 2)], at_x(-ex))
    share_same(6)

    arrived("GP2")
    send("GM3", gt.at[0, 1], gt.at[1, 2], z_last)
    arrived("GM2")
    send("GP3", gt.at[1, 1], gt.at[0, 2], z_first)
    send("A1P", xb.at[side], xb.at[8 + side], z_first)
    forward(2)
    forward(6)
    arrived("L2")
    send("L3", xb.at[mine], xb.at[OTHER + 4], z_last)

    @pl.when(middle == 1)
    def _():
        descriptor("A1M").start()
        relay(0, 0)

    arrived("S2")
    share_other(5)
    arrived("Y2")
    share_same(3)
    arrived("X2")
    share_same(7)

    arrived("GP3")
    send("GM4", gt.at[0, 2], gb.at[even, 2], z_last)
    arrived("GM3")
    send("GP4", gt.at[1, 2], gb.at[odd, 2], z_first)

    @pl.when(middle == 1)
    def _():
        relay(1, 0)

    forward(3)
    forward(7)
    arrived("L3")
    send("L4", xb.at[OTHER + 4], xb.at[OTHER + 0], z_first)
    share_other(4)
    arrived("A1P")

    @pl.when(middle == 1)
    def _():
        descriptor("A2M").start()

    share_same(4)
    arrived("GP4")

    @pl.when(middle == 1)
    def _():
        arrived("A1M")
        descriptor("A2P").start()

    @pl.when(end == 1)
    def _():
        arrived("GM4")
        relay(0, 2)
        relay(1, 2)
        descriptor("CH").start()

    forward(4)
    for s in (3, 7, 2, 6):
        arrived(f"B{s}")
        add_terms(TERM[s])

    arrived("L4")
    send("OY1", xb.at[OTHER + 0], xb.at[OTHER + 2], at_y(ey))
    send("OX1", xb.at[OTHER + 0], xb.at[OTHER + 6], at_x(ex))
    share_other(0)
    add_and_pass(0)

    @pl.when(middle == 1)
    def _():
        arrived("GM4")
        descriptor("CH").start()

    arrived("OY1")
    send("OY2", xb.at[OTHER + 2], xb.at[OTHER + 3], at_y(-ey))
    share_other(2)
    arrived("OX1")
    send("OX2", xb.at[OTHER + 6], xb.at[OTHER + 7], at_x(-ex))
    share_other(6)
    for name in ("C0", "CG", "CH", "D0"):
        arrived(name)
    weight_grad(0)
    add_and_pass(1)
    weight_grad(1)
    for s in (4, 2, 6):
        arrived(f"C{s}")
        arrived(f"D{s}")
        weight_grad(s)
    arrived("OY2")
    share_other(3)
    arrived("OX2")
    share_other(7)

    @pl.when(end == 1)
    def _():
        arrived("A2P")

    @pl.when(middle == 1)
    def _():
        arrived("A2M")

    share_same(5)
    forward(5)
    for r in range(2):
        out_ref[:, pl.ds(r * 512, 512)] = acc_o[r].astype(BF16)
    for s in (3, 7, 5):
        arrived(f"C{s}")
        arrived(f"D{s}")
        weight_grad(s)
    for r in range(2):
        arrived(f"Q{2 * r}")
        arrived(f"Q{2 * r + 1}")
        ig_ref[:, pl.ds(r * 512, 512)] = (acc_g[r] + rb[TERM[4], r].astype(F32)).astype(BF16)

    for name in NAMES:
        descriptor(name).wait_send()

    @pl.when(middle == 1)
    def _():
        for name in MIDDLE:
            descriptor(name).wait_send()


def settle(out_in, ig_in, dw_in, out_ref, ig_ref, dw_ref, sem):
    moves = []
    for r in range(2):
        for s in range(0, 8, 4):
            slots = pl.ds(s, 4)
            moves.append((dw_in.at[r, slots], dw_ref.at[r, slots]))
        rows = pl.ds(r * 128, 128)
        moves.append((out_in.at[rows], out_ref.at[rows]))
        moves.append((ig_in.at[rows], ig_ref.at[rows]))
    moves = [pltpu.make_async_copy(src, dst, sem.at[k]) for k, (src, dst) in enumerate(moves)]
    for move in moves:
        move.start()
    for move in moves:
        move.wait()


def body(inputs, weights, cotangent):
    n = len(NAMES + MIDDLE)
    results = pl.pallas_call(
        kernel,
        out_shape=(
            pltpu.VMEM((256, 1024), BF16),
            pltpu.VMEM((256, 1024), BF16),
            pltpu.VMEM((2, 8, 128, 512), BF16),
        ),
        in_specs=[pl.BlockSpec(memory_space=pl.ANY)] * 3,
        out_specs=[pl.BlockSpec(memory_space=pltpu.VMEM)] * 3,
        scratch_shapes=[
            pltpu.VMEM((24, 2, 2, 256, 128), BF16),
            pltpu.VMEM((8, 2, 2, 256, 128), BF16),
            pltpu.VMEM((8, 2, 512, 512), BF16),
            pltpu.VMEM((2, 4, 256, 512), BF16),
            pltpu.VMEM((2, 3, 256, 512), BF16),
            pltpu.VMEM((2, 2, 2, 256, 128), BF16),
            pltpu.VMEM((6, 2, 256, 512), BF16),
            pltpu.VMEM((6, 2, 256, 512), BF16),
            pltpu.VMEM((2, 256, 512), F32),
            pltpu.VMEM((2, 256, 512), F32),
            pltpu.SemaphoreType.DMA((n,)),
            pltpu.SemaphoreType.DMA((n,)),
            pltpu.SemaphoreType.DMA((8,)),
            pltpu.SemaphoreType.DMA((2,)),
            pltpu.SemaphoreType.DMA((8,)),
        ],
        compiler_params=pltpu.CompilerParams(
            collective_id=0, has_side_effects=True, vmem_limit_bytes=56 * 2**20
        ),
        cost_estimate=pl.CostEstimate(flops=6442450944, bytes_accessed=12 * 2**20, transcendentals=0),
    )(inputs, weights, cotangent)
    return pl.pallas_call(
        settle,
        out_shape=tuple(jax.ShapeDtypeStruct(result.shape, result.dtype) for result in results),
        in_specs=[pl.BlockSpec(memory_space=pl.ANY)] * 3,
        out_specs=[pl.BlockSpec(memory_space=pl.ANY)] * 3,
        scratch_shapes=[pltpu.SemaphoreType.DMA((8,))],
        compiler_params=pltpu.CompilerParams(vmem_limit_bytes=8 * 2**20),
    )(*results)


def solution(mesh):
    in_specs = (P("dp", "feat"), P("feat", None, None, None), P("dp", "feat"))
    out_specs = (P("dp", "feat"), P("dp", "feat"), P("feat", None, "dp", None))
    return jax.shard_map(body, mesh=mesh, in_specs=in_specs, out_specs=out_specs, check_vma=False)
```

```python
import jax
import jax.numpy as jnp
from jax import lax
from jax.experimental import pallas as pl
from jax.experimental.pallas import tpu as pltpu
from jax.sharding import PartitionSpec as P

MESH = pl.DeviceIdType.MESH
BF16 = jnp.bfloat16
F32 = jnp.float32
OTHER = 16
NAMES = (
    ["GP1", "GM1", "GP2", "GM2", "GP3", "GM3", "GP4", "GM4", "S1", "S2", "L1", "L2", "L3", "L4a", "L4b", "A1P"]
    + ["Y1", "Y2", "X1", "X2"]
    + [f"O{axis}{hop}{part}" for axis in "XY" for hop in (1, 2) for part in "ab"]
    + ["B2", "B3", "B6", "B7", "R0", "R1", "R2", "R3", "Q0", "Q1", "Q2", "Q3", "CG", "CH"]
    + [f"C{s}" for s in (0, 2, 3, 4, 5, 6, 7)]
    + [f"D{s}" for s in (0, 2, 3, 4, 5, 6, 7)]
)
MIDDLE = ["A1M", "A2P", "A2M"]
IDS = {name: number for number, name in enumerate(NAMES + MIDDLE)}
TERM = {2: 0, 3: 1, 6: 2, 7: 3, 5: 4, 4: 5}


def kernel(x_ref, w_ref, g_ref, out_ref, ig_ref, dw_ref, xb, sx, wb, gb, gt, at, rb, sb, acc_o, acc_g,
           send_sem, recv_sem, x_sem, g_sem, w_sem):
    feat = lax.axis_index("feat")
    dp = lax.axis_index("dp")
    y = feat % 4
    z_lo = (feat // 4) % 4
    x = feat // 16
    side = dp // 2
    core = dp % 2
    z = side * 4 + z_lo
    ey = 1 - 2 * (y % 2)
    ex = 1 - 2 * (x % 2)
    ez = 1 - 2 * (z % 2)
    middle = ((z_lo + 1) // 2) % 2
    end = 1 - middle
    away = 1 - side

    def at_y(step):
        return (x * 16 + z_lo * 4 + (y + step + 4) % 4, dp)

    def at_x(step):
        return (((x + step + 4) % 4) * 16 + z_lo * 4 + y, dp)

    def at_z(step):
        there = (z + step + 8) % 8
        return (x * 16 + (there % 4) * 4 + y, (there // 4) * 2 + core)

    sibling = (feat, side * 2 + 1 - core)
    z_first = at_z(ez)
    z_last = at_z(-ez)
    odd = z % 2
    even = 1 - odd
    second = end * (OTHER + 5) + middle * (10 + away)
    mine = middle * (OTHER + 5) + end * (10 + away)

    barrier = pltpu.get_barrier_semaphore()
    friends = [sibling, at_z(1), at_z(-1), at_y(1), at_y(-1), at_y(2), at_x(1), at_x(-1), at_x(2)]
    for friend in friends:
        pl.semaphore_signal(barrier, inc=1, device_id=friend, device_id_type=MESH)
    g_loads = []
    for r in range(2):
        load = pltpu.make_async_copy(g_ref.at[:, pl.ds(r * 512, 512)], gb.at[r, 0], g_sem.at[r])
        load.start()
        g_loads.append(load)
    loads = []
    for d in range(4):
        for r in range(2):
            load = pltpu.make_async_copy(
                x_ref.at[:, pl.ds(r * 512 + d * 128, 128)], xb.at[d // 2, d % 2, r], x_sem.at[d * 2 + r]
            )
            load.start()
            loads.append(load)
    pl.semaphore_wait(barrier, len(friends))

    routes = {}

    def descriptor(name):
        src, dst, device = routes[name]
        return pltpu.make_async_remote_copy(
            src_ref=src, dst_ref=dst, send_sem=send_sem.at[IDS[name]], recv_sem=recv_sem.at[IDS[name]],
            device_id=device, device_id_type=MESH,
        )

    def send(name, src, dst, device):
        routes[name] = (src, dst, device)
        descriptor(name).start()

    def arrived(name):
        descriptor(name).wait_recv()

    def send_half(name, here, there, part, device):
        column = 1 - core if part == "a" else core
        send(name + part, xb.at[OTHER + here, column], xb.at[OTHER + there, column], device)

    def share_same(s):
        send(f"C{s}", xb.at[2 * s + side, 1 - core], sx.at[s, 0], sibling)

    def share_other(s):
        send(f"D{s}", xb.at[OTHER + s, 1 - core], sx.at[s, 1], sibling)

    def forward(s, start=False):
        base = 0 if s == 1 else 2 * s

        def row(r, carry):
            k = 1 - r if s == 1 else r
            block = jnp.concatenate([xb[base + d // 2, d % 2, k] for d in range(4)], axis=1)
            part = jnp.dot(block, wb[s, r], preferred_element_type=F32)
            if start:
                acc_o[r] = part
            else:
                acc_o[r] += part
            return carry

        lax.fori_loop(0, 2, row, 0)

    def term(s, r, q=0):
        return lax.dot_general(gb[r, q], wb[s, r], (((1,), (1,)), ((), ())), preferred_element_type=F32)

    def back(s):
        def row(r, carry):
            sb[TERM[s], r] = term(s, r).astype(BF16)
            return carry

        lax.fori_loop(0, 2, row, 0)

    def back_local():
        def row(r, carry):
            acc_g[r] = term(0, r) + term(1, 1 - r).astype(BF16).astype(F32)
            return carry

        lax.fori_loop(0, 2, row, 0)

    def add_terms(k):
        def row(r, carry):
            acc_g[r] += rb[k, r].astype(F32)
            return carry

        lax.fori_loop(0, 2, row, 0)

    for r in range(2):
        for h in range(2):
            rows = pl.ds(h * 128, 128)
            routes[f"R{2 * r + h}"] = (sb.at[TERM[5], r, rows], rb.at[TERM[5], r, rows], z_last)
            routes[f"Q{2 * r + h}"] = (sb.at[TERM[4], r, rows], rb.at[TERM[4], r, rows], z_first)

    def relay(r, q):
        sb[TERM[5], r] = term(5, r, q).astype(BF16)
        for h in range(2):
            descriptor(f"R{2 * r + h}").start()

    def add_and_pass(r):
        for h in range(2):
            rows = pl.ds(h * 128, 128)
            arrived(f"R{2 * r + h}")
            total = sb[TERM[4], r, rows].astype(F32) + rb[TERM[5], r, rows].astype(F32)
            sb[TERM[4], r, rows] = total.astype(BF16)
            descriptor(f"Q{2 * r + h}").start()

    def weight_grad(s):
        base = 0 if s == 1 else s

        def row(r, carry):
            k = 1 - r if s == 1 else r
            tokens = jnp.concatenate(
                [xb[2 * base + side, core, k], sx[base, 0, k], xb[OTHER + base, core, k], sx[base, 1, k]], axis=0
            )
            total = lax.dot_general(
                tokens, gb[r].reshape(1024, 512), (((0,), (0,)), ((), ())), preferred_element_type=F32
            )
            dw_ref[r, s] = total.astype(BF16)
            return carry

        lax.fori_loop(0, 2, row, 0)

    routes["CH"] = (gb.at[:, 2], gb.at[:, 3], sibling)
    routes["A1M"] = (xb.at[side], at.at[1], z_last)
    routes["A2P"] = (at.at[1], xb.at[10 + side], z_first)
    routes["A2M"] = (xb.at[8 + side], xb.at[10 + side], z_last)

    for load in g_loads:
        load.wait()
    send("GP1", gb.at[odd, 0], gt.at[0, 0], z_first)
    send("GM1", gb.at[even, 0], gt.at[1, 0], z_last)
    for load in loads:
        load.wait()
    send("S1", xb.at[away], xb.at[8 + away], z_first)
    send("L1", xb.at[away], at.at[0], z_last)
    send("Y1", xb.at[pl.ds(0, 2)], xb.at[pl.ds(4, 2)], at_y(ey))
    send("X1", xb.at[pl.ds(0, 2)], xb.at[pl.ds(12, 2)], at_x(ex))
    share_same(0)
    send("CG", gb.at[:, 0], gb.at[:, 1], sibling)
    w_loads = {}
    for s in (3, 7, 2, 6, 0, 1, 4, 5):
        w_loads[s] = pltpu.make_async_copy(w_ref.at[:, s], wb.at[s], w_sem.at[s])
        w_loads[s].start()

    for s, device in ((3, at_y(2)), (7, at_x(2)), (2, at_y(ey)), (6, at_x(ex))):
        w_loads[s].wait()
        back(s)
        send(f"B{s}", sb.at[TERM[s]], rb.at[TERM[s]], device)
    for s in (5, 4, 0, 1):
        w_loads[s].wait()

    arrived("GP1")
    send("GM2", gt.at[0, 0], gt.at[1, 1], z_last)
    arrived("GM1")
    send("GP2", gt.at[1, 0], gt.at[0, 1], z_first)
    forward(0, start=True)
    forward(1)
    arrived("S1")
    send("S2", xb.at[8 + away], xb.at[second], z_last)
    arrived("L1")
    send("L2", at.at[0], xb.at[second], z_first)
    back_local()
    back(4)
    arrived("Y1")
    send("Y2", xb.at[pl.ds(4, 2)], xb.at[pl.ds(6, 2)], at_y(-ey))
    share_same(2)
    arrived("X1")
    send("X2", xb.at[pl.ds(12, 2)], xb.at[pl.ds(14, 2)], at_x(-ex))
    share_same(6)

    arrived("GP2")
    send("GM3", gt.at[0, 1], gt.at[1, 2], z_last)
    arrived("GM2")
    send("GP3", gt.at[1, 1], gt.at[0, 2], z_first)
    send("A1P", xb.at[side], xb.at[8 + side], z_first)
    forward(2)
    forward(6)
    arrived("L2")
    send("L3", xb.at[mine], xb.at[OTHER + 4], z_last)

    @pl.when(middle == 1)
    def _():
        descriptor("A1M").start()
        relay(0, 0)

    arrived("S2")
    share_other(5)
    arrived("Y2")
    share_same(3)
    arrived("X2")
    share_same(7)

    arrived("GP3")
    send("GM4", gt.at[0, 2], gb.at[even, 2], z_last)
    arrived("GM3")
    send("GP4", gt.at[1, 2], gb.at[odd, 2], z_first)

    @pl.when(middle == 1)
    def _():
        relay(1, 0)

    forward(3)
    forward(7)
    arrived("L3")
    send_half("L4", 4, 0, "a", z_first)
    send_half("L4", 4, 0, "b", z_first)
    share_other(4)
    arrived("A1P")

    @pl.when(middle == 1)
    def _():
        descriptor("A2M").start()

    share_same(4)
    arrived("GP4")

    @pl.when(middle == 1)
    def _():
        arrived("A1M")
        descriptor("A2P").start()

    @pl.when(end == 1)
    def _():
        arrived("GM4")
        relay(0, 2)
        relay(1, 2)
        descriptor("CH").start()

    forward(4)
    for s in (3, 7, 2, 6):
        arrived(f"B{s}")
        add_terms(TERM[s])

    for part in "ab":
        arrived(f"L4{part}")
        send_half("OY1", 0, 2, part, at_y(ey))
        send_half("OX1", 0, 6, part, at_x(ex))
        if part == "a":
            share_other(0)
    add_and_pass(0)

    @pl.when(middle == 1)
    def _():
        arrived("GM4")
        descriptor("CH").start()

    for part in "ab":
        arrived(f"OY1{part}")
        send_half("OY2", 2, 3, part, at_y(-ey))
        arrived(f"OX1{part}")
        send_half("OX2", 6, 7, part, at_x(-ex))
        if part == "a":
            share_other(2)
            share_other(6)
    for name in ("C0", "CG", "CH", "D0"):
        arrived(name)
    weight_grad(0)
    add_and_pass(1)
    weight_grad(1)
    for s in (4, 2, 6):
        arrived(f"C{s}")
        arrived(f"D{s}")
        weight_grad(s)
    arrived("OY2a")
    share_other(3)
    arrived("OX2a")
    share_other(7)
    arrived("OY2b")
    arrived("OX2b")

    @pl.when(end == 1)
    def _():
        arrived("A2P")

    @pl.when(middle == 1)
    def _():
        arrived("A2M")

    share_same(5)
    forward(5)
    for r in range(2):
        out_ref[:, pl.ds(r * 512, 512)] = acc_o[r].astype(BF16)
    for s in (3, 7, 5):
        arrived(f"C{s}")
        arrived(f"D{s}")
        weight_grad(s)
    for r in range(2):
        arrived(f"Q{2 * r}")
        arrived(f"Q{2 * r + 1}")
        ig_ref[:, pl.ds(r * 512, 512)] = (acc_g[r] + rb[TERM[4], r].astype(F32)).astype(BF16)

    for name in NAMES:
        descriptor(name).wait_send()

    @pl.when(middle == 1)
    def _():
        for name in MIDDLE:
            descriptor(name).wait_send()


def settle(out_in, ig_in, dw_in, out_ref, ig_ref, dw_ref, sem):
    moves = []
    for r in range(2):
        for s in range(0, 8, 4):
            slots = pl.ds(s, 4)
            moves.append((dw_in.at[r, slots], dw_ref.at[r, slots]))
        rows = pl.ds(r * 128, 128)
        moves.append((out_in.at[rows], out_ref.at[rows]))
        moves.append((ig_in.at[rows], ig_ref.at[rows]))
    moves = [pltpu.make_async_copy(src, dst, sem.at[k]) for k, (src, dst) in enumerate(moves)]
    for move in moves:
        move.start()
    for move in moves:
        move.wait()


def body(inputs, weights, cotangent):
    n = len(NAMES + MIDDLE)
    results = pl.pallas_call(
        kernel,
        out_shape=(
            pltpu.VMEM((256, 1024), BF16),
            pltpu.VMEM((256, 1024), BF16),
            pltpu.VMEM((2, 8, 128, 512), BF16),
        ),
        in_specs=[pl.BlockSpec(memory_space=pl.ANY)] * 3,
        out_specs=[pl.BlockSpec(memory_space=pltpu.VMEM)] * 3,
        scratch_shapes=[
            pltpu.VMEM((24, 2, 2, 256, 128), BF16),
            pltpu.VMEM((8, 2, 2, 256, 128), BF16),
            pltpu.VMEM((8, 2, 512, 512), BF16),
            pltpu.VMEM((2, 4, 256, 512), BF16),
            pltpu.VMEM((2, 3, 256, 512), BF16),
            pltpu.VMEM((2, 2, 2, 256, 128), BF16),
            pltpu.VMEM((6, 2, 256, 512), BF16),
            pltpu.VMEM((6, 2, 256, 512), BF16),
            pltpu.VMEM((2, 256, 512), F32),
            pltpu.VMEM((2, 256, 512), F32),
            pltpu.SemaphoreType.DMA((n,)),
            pltpu.SemaphoreType.DMA((n,)),
            pltpu.SemaphoreType.DMA((8,)),
            pltpu.SemaphoreType.DMA((2,)),
            pltpu.SemaphoreType.DMA((8,)),
        ],
        compiler_params=pltpu.CompilerParams(
            collective_id=0, has_side_effects=True, vmem_limit_bytes=56 * 2**20
        ),
        cost_estimate=pl.CostEstimate(flops=6442450944, bytes_accessed=12 * 2**20, transcendentals=0),
    )(inputs, weights, cotangent)
    return pl.pallas_call(
        settle,
        out_shape=tuple(jax.ShapeDtypeStruct(result.shape, result.dtype) for result in results),
        in_specs=[pl.BlockSpec(memory_space=pl.ANY)] * 3,
        out_specs=[pl.BlockSpec(memory_space=pl.ANY)] * 3,
        scratch_shapes=[pltpu.SemaphoreType.DMA((8,))],
        compiler_params=pltpu.CompilerParams(vmem_limit_bytes=8 * 2**20),
    )(*results)


def solution(mesh):
    in_specs = (P("dp", "feat"), P("feat", None, None, None), P("dp", "feat"))
    out_specs = (P("dp", "feat"), P("dp", "feat"), P("feat", None, "dp", None))
    return jax.shard_map(body, mesh=mesh, in_specs=in_specs, out_specs=out_specs, check_vma=False)
```

```python
import jax
import jax.numpy as jnp
from jax import lax
from jax.experimental import pallas as pl
from jax.experimental.pallas import tpu as pltpu
from jax.sharding import PartitionSpec as P

MESH = pl.DeviceIdType.MESH
BF16 = jnp.bfloat16
F32 = jnp.float32
OTHER = 16
NAMES = (
    ["GP1", "GM1", "GP2", "GM2", "GP3", "GM3", "GP4", "GM4", "S1", "S2", "L1", "L2", "L3", "L4a", "L4b", "A1P"]
    + ["Y1", "Y2", "X1", "X2"]
    + [f"O{axis}{hop}{part}" for axis in "XY" for hop in (1, 2) for part in "ab"]
    + ["B2", "B3", "B6", "B7", "R0", "R1", "R2", "R3", "Q0", "Q1", "Q2", "Q3", "CG", "CH"]
    + [f"C{s}" for s in (0, 2, 3, 4, 5, 6, 7)]
    + [f"D{s}" for s in (0, 2, 3, 4, 5, 6, 7)]
)
MIDDLE = ["A1M", "A2P", "A2M"]
IDS = {name: number for number, name in enumerate(NAMES + MIDDLE)}
TERM = {2: 0, 3: 1, 6: 2, 7: 3, 5: 4, 4: 5}


def kernel(x_ref, w_ref, g_ref, out_ref, ig_ref, dw_ref, xb, sx, wb, gb, gt, at, rb, sb, acc_o, acc_g,
           send_sem, recv_sem, x_sem, g_sem, w_sem):
    feat = lax.axis_index("feat")
    dp = lax.axis_index("dp")
    y = feat % 4
    z_lo = (feat // 4) % 4
    x = feat // 16
    side = dp // 2
    core = dp % 2
    z = side * 4 + z_lo
    ey = 1 - 2 * (y % 2)
    ex = 1 - 2 * (x % 2)
    ez = 1 - 2 * (z % 2)
    middle = ((z_lo + 1) // 2) % 2
    end = 1 - middle
    away = 1 - side

    def at_y(step):
        return (x * 16 + z_lo * 4 + (y + step + 4) % 4, dp)

    def at_x(step):
        return (((x + step + 4) % 4) * 16 + z_lo * 4 + y, dp)

    def at_z(step):
        there = (z + step + 8) % 8
        return (x * 16 + (there % 4) * 4 + y, (there // 4) * 2 + core)

    sibling = (feat, side * 2 + 1 - core)
    z_first = at_z(ez)
    z_last = at_z(-ez)
    odd = z % 2
    even = 1 - odd
    second = end * (OTHER + 5) + middle * (10 + away)
    mine = middle * (OTHER + 5) + end * (10 + away)

    barrier = pltpu.get_barrier_semaphore()
    friends = [sibling, at_z(1), at_z(-1), at_y(1), at_y(-1), at_y(2), at_x(1), at_x(-1), at_x(2)]
    for friend in friends:
        pl.semaphore_signal(barrier, inc=1, device_id=friend, device_id_type=MESH)
    g_loads = []
    for r in range(2):
        load = pltpu.make_async_copy(g_ref.at[:, pl.ds(r * 512, 512)], gb.at[r, 0], g_sem.at[r])
        load.start()
        g_loads.append(load)
    loads = []
    for d in range(4):
        for r in range(2):
            load = pltpu.make_async_copy(
                x_ref.at[:, pl.ds(r * 512 + d * 128, 128)], xb.at[d // 2, d % 2, r], x_sem.at[d * 2 + r]
            )
            load.start()
            loads.append(load)
    pl.semaphore_wait(barrier, len(friends))

    routes = {}

    def descriptor(name):
        src, dst, device = routes[name]
        return pltpu.make_async_remote_copy(
            src_ref=src, dst_ref=dst, send_sem=send_sem.at[IDS[name]], recv_sem=recv_sem.at[IDS[name]],
            device_id=device, device_id_type=MESH,
        )

    def send(name, src, dst, device):
        routes[name] = (src, dst, device)
        descriptor(name).start()

    def arrived(name):
        descriptor(name).wait_recv()

    def send_half(name, here, there, part, device):
        column = 1 - core if part == "a" else core
        send(name + part, xb.at[OTHER + here, column], xb.at[OTHER + there, column], device)

    def share_same(s):
        send(f"C{s}", xb.at[2 * s + side, 1 - core], sx.at[s, 0], sibling)

    def share_other(s):
        send(f"D{s}", xb.at[OTHER + s, 1 - core], sx.at[s, 1], sibling)

    def forward(s, start=False):
        base = 0 if s == 1 else 2 * s

        def row(r, carry):
            k = 1 - r if s == 1 else r
            block = jnp.concatenate([xb[base + d // 2, d % 2, k] for d in range(4)], axis=1)
            part = jnp.dot(block, wb[s, r], preferred_element_type=F32)
            if start:
                acc_o[r] = part
            else:
                acc_o[r] += part
            return carry

        lax.fori_loop(0, 2, row, 0)

    def term(s, r, q=0):
        return lax.dot_general(gb[r, q], wb[s, r], (((1,), (1,)), ((), ())), preferred_element_type=F32)

    def back(s):
        def row(r, carry):
            sb[TERM[s], r] = term(s, r).astype(BF16)
            return carry

        lax.fori_loop(0, 2, row, 0)

    def back_local():
        def row(r, carry):
            acc_g[r] = term(0, r) + term(1, 1 - r).astype(BF16).astype(F32)
            return carry

        lax.fori_loop(0, 2, row, 0)

    def add_terms(k):
        def row(r, carry):
            acc_g[r] += rb[k, r].astype(F32)
            return carry

        lax.fori_loop(0, 2, row, 0)

    for r in range(2):
        for h in range(2):
            rows = pl.ds(h * 128, 128)
            routes[f"R{2 * r + h}"] = (sb.at[TERM[5], r, rows], rb.at[TERM[5], r, rows], z_last)
            routes[f"Q{2 * r + h}"] = (sb.at[TERM[4], r, rows], rb.at[TERM[4], r, rows], z_first)

    def relay(r, q):
        sb[TERM[5], r] = term(5, r, q).astype(BF16)
        for h in range(2):
            descriptor(f"R{2 * r + h}").start()

    def add_and_pass(r):
        for h in range(2):
            rows = pl.ds(h * 128, 128)
            arrived(f"R{2 * r + h}")
            total = sb[TERM[4], r, rows].astype(F32) + rb[TERM[5], r, rows].astype(F32)
            sb[TERM[4], r, rows] = total.astype(BF16)
            descriptor(f"Q{2 * r + h}").start()

    def weight_grad(s):
        base = 0 if s == 1 else s

        def row(r, carry):
            k = 1 - r if s == 1 else r
            tokens = jnp.concatenate(
                [xb[2 * base + side, core, k], sx[base, 0, k], xb[OTHER + base, core, k], sx[base, 1, k]], axis=0
            )
            total = lax.dot_general(
                tokens, gb[r].reshape(1024, 512), (((0,), (0,)), ((), ())), preferred_element_type=F32
            )
            dw_ref[r, s] = total.astype(BF16)
            return carry

        lax.fori_loop(0, 2, row, 0)

    routes["CH"] = (gb.at[:, 2], gb.at[:, 3], sibling)
    routes["A1M"] = (xb.at[side], at.at[1], z_last)
    routes["A2P"] = (at.at[1], xb.at[10 + side], z_first)
    routes["A2M"] = (xb.at[8 + side], xb.at[10 + side], z_last)

    for load in g_loads:
        load.wait()
    send("GP1", gb.at[odd, 0], gt.at[0, 0], z_first)
    send("GM1", gb.at[even, 0], gt.at[1, 0], z_last)
    for load in loads:
        load.wait()
    send("S1", xb.at[away], xb.at[8 + away], z_first)
    send("L1", xb.at[away], at.at[0], z_last)
    send("Y1", xb.at[pl.ds(0, 2)], xb.at[pl.ds(4, 2)], at_y(ey))
    send("X1", xb.at[pl.ds(0, 2)], xb.at[pl.ds(12, 2)], at_x(ex))
    share_same(0)
    send("CG", gb.at[:, 0], gb.at[:, 1], sibling)
    w_loads = {}
    for s in (3, 7, 2, 6, 0, 1, 4, 5):
        w_loads[s] = pltpu.make_async_copy(w_ref.at[:, s], wb.at[s], w_sem.at[s])
        w_loads[s].start()

    for s, device in ((3, at_y(2)), (7, at_x(2)), (2, at_y(ey)), (6, at_x(ex))):
        w_loads[s].wait()
        back(s)
        send(f"B{s}", sb.at[TERM[s]], rb.at[TERM[s]], device)
    for s in (5, 4, 0, 1):
        w_loads[s].wait()

    arrived("GP1")
    send("GM2", gt.at[0, 0], gt.at[1, 1], z_last)
    arrived("GM1")
    send("GP2", gt.at[1, 0], gt.at[0, 1], z_first)
    forward(0, start=True)
    forward(1)
    arrived("S1")
    send("S2", xb.at[8 + away], xb.at[second], z_last)
    arrived("L1")
    send("L2", at.at[0], xb.at[second], z_first)
    back_local()
    back(4)
    arrived("Y1")
    send("Y2", xb.at[pl.ds(4, 2)], xb.at[pl.ds(6, 2)], at_y(-ey))
    share_same(2)
    arrived("X1")
    send("X2", xb.at[pl.ds(12, 2)], xb.at[pl.ds(14, 2)], at_x(-ex))
    share_same(6)

    arrived("GP2")
    send("GM3", gt.at[0, 1], gt.at[1, 2], z_last)
    arrived("GM2")
    send("GP3", gt.at[1, 1], gt.at[0, 2], z_first)
    send("A1P", xb.at[side], xb.at[8 + side], z_first)
    forward(2)
    forward(6)
    arrived("L2")
    send("L3", xb.at[mine], xb.at[OTHER + 4], z_last)

    @pl.when(middle == 1)
    def _():
        descriptor("A1M").start()
        relay(0, 0)

    arrived("S2")
    share_other(5)
    arrived("Y2")
    share_same(3)
    arrived("X2")
    share_same(7)

    arrived("GP3")
    send("GM4", gt.at[0, 2], gb.at[even, 2], z_last)
    arrived("GM3")
    send("GP4", gt.at[1, 2], gb.at[odd, 2], z_first)

    @pl.when(middle == 1)
    def _():
        relay(1, 0)

    forward(3)
    forward(7)
    arrived("L3")
    send_half("L4", 4, 0, "a", z_first)
    send_half("L4", 4, 0, "b", z_first)
    share_other(4)
    arrived("A1P")

    @pl.when(middle == 1)
    def _():
        descriptor("A2M").start()

    share_same(4)
    arrived("GP4")

    @pl.when(middle == 1)
    def _():
        arrived("A1M")
        descriptor("A2P").start()

    @pl.when(end == 1)
    def _():
        arrived("GM4")
        relay(0, 2)
        relay(1, 2)
        descriptor("CH").start()

    forward(4)
    for s in (3, 7, 2, 6):
        arrived(f"B{s}")
        add_terms(TERM[s])

    for part in "ab":
        arrived(f"L4{part}")
        send_half("OY1", 0, 2, part, at_y(ey))
        send_half("OX1", 0, 6, part, at_x(ex))
        if part == "a":
            share_other(0)
    add_and_pass(0)

    @pl.when(middle == 1)
    def _():
        arrived("GM4")
        descriptor("CH").start()

    for part in "ab":
        arrived(f"OY1{part}")
        send_half("OY2", 2, 3, part, at_y(-ey))
        arrived(f"OX1{part}")
        send_half("OX2", 6, 7, part, at_x(-ex))
        if part == "a":
            share_other(2)
            share_other(6)
    for name in ("C0", "CG", "CH", "D0"):
        arrived(name)
    weight_grad(0)
    add_and_pass(1)
    weight_grad(1)
    arrived("C4")
    arrived("D4")
    weight_grad(4)
    arrived("OY2a")
    share_other(3)
    arrived("OX2a")
    share_other(7)
    for s in (2, 6):
        arrived(f"C{s}")
        arrived(f"D{s}")
        weight_grad(s)
    arrived("OY2b")
    arrived("OX2b")

    @pl.when(end == 1)
    def _():
        arrived("A2P")

    @pl.when(middle == 1)
    def _():
        arrived("A2M")

    share_same(5)
    forward(5)
    for r in range(2):
        out_ref[:, pl.ds(r * 512, 512)] = acc_o[r].astype(BF16)
    for s in (3, 7, 5):
        arrived(f"C{s}")
        arrived(f"D{s}")
        weight_grad(s)
    for r in range(2):
        arrived(f"Q{2 * r}")
        arrived(f"Q{2 * r + 1}")
        ig_ref[:, pl.ds(r * 512, 512)] = (acc_g[r] + rb[TERM[4], r].astype(F32)).astype(BF16)

    for name in NAMES:
        descriptor(name).wait_send()

    @pl.when(middle == 1)
    def _():
        for name in MIDDLE:
            descriptor(name).wait_send()


def settle(out_in, ig_in, dw_in, out_ref, ig_ref, dw_ref, sem):
    moves = []
    for r in range(2):
        for s in range(0, 8, 4):
            slots = pl.ds(s, 4)
            moves.append((dw_in.at[r, slots], dw_ref.at[r, slots]))
        rows = pl.ds(r * 128, 128)
        moves.append((out_in.at[rows], out_ref.at[rows]))
        moves.append((ig_in.at[rows], ig_ref.at[rows]))
    moves = [pltpu.make_async_copy(src, dst, sem.at[k]) for k, (src, dst) in enumerate(moves)]
    for move in moves:
        move.start()
    for move in moves:
        move.wait()


def body(inputs, weights, cotangent):
    n = len(NAMES + MIDDLE)
    results = pl.pallas_call(
        kernel,
        out_shape=(
            pltpu.VMEM((256, 1024), BF16),
            pltpu.VMEM((256, 1024), BF16),
            pltpu.VMEM((2, 8, 128, 512), BF16),
        ),
        in_specs=[pl.BlockSpec(memory_space=pl.ANY)] * 3,
        out_specs=[pl.BlockSpec(memory_space=pltpu.VMEM)] * 3,
        scratch_shapes=[
            pltpu.VMEM((24, 2, 2, 256, 128), BF16),
            pltpu.VMEM((8, 2, 2, 256, 128), BF16),
            pltpu.VMEM((8, 2, 512, 512), BF16),
            pltpu.VMEM((2, 4, 256, 512), BF16),
            pltpu.VMEM((2, 3, 256, 512), BF16),
            pltpu.VMEM((2, 2, 2, 256, 128), BF16),
            pltpu.VMEM((6, 2, 256, 512), BF16),
            pltpu.VMEM((6, 2, 256, 512), BF16),
            pltpu.VMEM((2, 256, 512), F32),
            pltpu.VMEM((2, 256, 512), F32),
            pltpu.SemaphoreType.DMA((n,)),
            pltpu.SemaphoreType.DMA((n,)),
            pltpu.SemaphoreType.DMA((8,)),
            pltpu.SemaphoreType.DMA((2,)),
            pltpu.SemaphoreType.DMA((8,)),
        ],
        compiler_params=pltpu.CompilerParams(
            collective_id=0, has_side_effects=True, vmem_limit_bytes=56 * 2**20
        ),
        cost_estimate=pl.CostEstimate(flops=6442450944, bytes_accessed=12 * 2**20, transcendentals=0),
    )(inputs, weights, cotangent)
    return pl.pallas_call(
        settle,
        out_shape=tuple(jax.ShapeDtypeStruct(result.shape, result.dtype) for result in results),
        in_specs=[pl.BlockSpec(memory_space=pl.ANY)] * 3,
        out_specs=[pl.BlockSpec(memory_space=pl.ANY)] * 3,
        scratch_shapes=[pltpu.SemaphoreType.DMA((8,))],
        compiler_params=pltpu.CompilerParams(vmem_limit_bytes=8 * 2**20),
    )(*results)


def solution(mesh):
    in_specs = (P("dp", "feat"), P("feat", None, None, None), P("dp", "feat"))
    out_specs = (P("dp", "feat"), P("dp", "feat"), P("feat", None, "dp", None))
    return jax.shard_map(body, mesh=mesh, in_specs=in_specs, out_specs=out_specs, check_vma=False)
```
